32 devices in a mesh: grp: 2 (over y), bond: 4 (over z), ops: 4 (over x, core).
Axes of the slice: x: 2, y: 2, z: 4, core: 2. Of those that a mesh axis runs over, the one named last changes fastest.
Arguments:
- wavefunction: bfloat16 [16, 16, 128, 128], P(('grp', 'bond'), 'ops'), parts along dimension 0, may hold values from -6 to 6
- left_blocks: bfloat16 [64, 8, 128, 128], P(('grp', 'ops'), 'bond'), parts along dimension 0, may hold values from -0.5 to 0.5
- right_blocks: bfloat16 [64, 8, 128, 128], P(('grp', 'ops'), 'bond'), parts along dimension 0, may hold values from -0.5 to 0.5
- site_blocks: float32 [64, 16, 16], P(('grp', 'ops')), parts along dimension 0, may hold values from -0.4375 to 0.4375
- preconditioner: float32 [16, 16, 128, 128], P(('grp', 'bond'), 'ops'), parts along dimension 0, may hold values from 0.5 to 4
- left_lengths: int32 [16], P(('grp', 'bond')), parts along dimension 0, may hold values from 1 to 128, 768 in all
- right_lengths: int32 [16], P(('grp', 'bond')), parts along dimension 0, may hold values from 1 to 128, 768 in all
- term_shift: int32 [64], P(('grp', 'ops')), parts along dimension 0, may hold values from -1 to 1
Outputs:
- first_sigma: float32 [16, 16, 128, 128], P(('grp', 'bond'), 'ops'), parts along dimension 0
- second_sigma: float32 [16, 16, 128, 128], P(('grp', 'bond'), 'ops'), parts along dimension 0
The draws below stay inside these ranges and needn't reach their ends.
There are 2 independent parts, one for each index of `grp`. The reference program is written for one: setup_inputs(seed, part) draws one part's arguments, and reference() takes and returns one part's arrays. A program takes and returns all parts, laid end to end along the dimension named above; each array names one. Nothing has to cross between parts.
Inputs may be any that keep to these rules, and one draw needn't show every extreme that they name: `left_lengths`: the lengths of one array sum to 8 * (96) and the largest is exactly 128. `right_lengths`: the lengths of one array sum to 8 * (96) and the largest is exactly 128.
All inputs are finite; a program needn't handle non-finite values. No bound on the sum of `left_lengths` or of `right_lengths` on one device may be relied on, other than what follows from the above.
Results may differ from the reference program's by a relative error of at most 0.018.
Values may be sent and summed in bfloat16 or wider, within the bound.
A program may use at most 64 MiB of HBM per device.

```python
import math
import jax
import jax.numpy as jnp
import numpy as np
from jax import lax

P_SIZE = 16
B = 128
TERM_DEV = 8
NS = 8
TERMS = 32
N_OPS = 4


def with_ends(entries, own_key, low, high):
    extent = entries.shape
    spot = [jax.random.randint(jax.random.fold_in(own_key, axis), (), 0, extent[axis]) for axis in range(len(extent))]
    entries = entries.at[tuple(spot)].set(low)
    longest = extent.index(max(extent))
    spot[longest] = (spot[longest] + 1) % extent[longest]
    return entries.at[tuple(spot)].set(high)


def block_scale(key, extent, shards, smallest, high):
    def one(dim, blocks):
        heights = jax.random.uniform(jax.random.fold_in(jax.random.fold_in(key, 6), dim), (blocks,), jnp.float32, smallest / len(shards), high / len(shards))
        return jnp.repeat(jnp.exp(heights), extent[dim] // blocks).reshape((-1,) + (1,) * (len(extent) - dim - 1))

    level = one(*shards[0])
    for cut in shards[1:]:
        level = level * one(*cut)
    return level


def split_up(count, total, limit, lean):
    weights = [(1 << 20) // math.isqrt(standing ** lean) + 1 for standing in range(2, count + 1)]
    spare, holding = total - limit - (count - 1), [1] * (count - 1)
    while spare > 0:
        movable = [i for i in range(count - 1) if holding[i] < limit]
        pool, remaining = sum([weights[i] for i in movable]), spare
        for i in movable:
            extra = min(limit - holding[i], max(1, remaining * weights[i] // pool), spare)
            holding[i] = holding[i] + extra
            spare = spare - extra
    return np.array([limit] + holding)


def uneven_parts(stream_key, amount, total, limit, skew):
    if amount == 2:
        one = jax.random.randint(stream_key, (), max(1, total - limit), min(limit, total - 1) + 1)
        return jnp.stack([one, total - one])
    lengths = jnp.asarray(split_up(amount, total, limit, skew), jnp.int32)
    twos = (amount - 1) // 2
    giver, taker = lengths[1:1 + 2 * twos:2], lengths[2:2 + 2 * twos:2]
    room = jnp.minimum(giver - 1, limit - taker)
    moved = jax.random.randint(jax.random.fold_in(stream_key, 1), (twos,), 0, 1 << 20) % (room + 1)
    lengths = lengths.at[1:1 + 2 * twos:2].set(giver - moved).at[2:2 + 2 * twos:2].set(taker + moved)
    return lengths[jax.random.permutation(jax.random.fold_in(stream_key, 2), amount)]


def centred(stream_key, dims, width, bound, shards=(), held_as=jnp.bfloat16):
    loudness = block_scale(stream_key, dims, shards, -0.22, 0.18) if shards else 1.0
    entries = jax.random.normal(stream_key, dims, jnp.float32) * width * loudness
    return jnp.minimum(jnp.maximum(entries, -bound), bound).astype(held_as)


def setup_inputs(seed: int = 0, part: int = 0) -> dict:
    key_list = jax.random.split(jax.random.key(seed), 9)
    part_keys = jax.random.split(jax.random.fold_in(key_list[8], part), 9)
    wavefunction = centred(part_keys[0], (NS, P_SIZE, B, B), 1.0, 6.0, ((0, 4), (1, 4)))
    left_blocks = centred(part_keys[1], (TERMS, NS, B, B), B ** -0.5, 0.5, ((0, 4), (1, 4)))
    right_blocks = centred(part_keys[2], (TERMS, NS, B, B), B ** -0.5, 0.5, ((0, 4), (1, 4)))
    site_blocks = centred(part_keys[3], (TERMS, P_SIZE, P_SIZE), (P_SIZE * TERMS // 3) ** -0.5, 0.4375, ((0, 4),), jnp.float32)
    preconditioner = jnp.clip(jnp.exp(math.log(4.0) - 2.0794415 * jax.random.uniform(part_keys[4], (NS, P_SIZE, B, B), jnp.float32) ** block_scale(part_keys[4], (NS, P_SIZE, B, B), ((0, 4), (1, 4)), -0.2, 0.2)), 0.5, 4.0)
    left_lengths = uneven_parts(part_keys[5], NS, NS * (3 * B // 4), B, 2).astype(jnp.int32)
    right_lengths = uneven_parts(part_keys[6], NS, NS * (3 * B // 4), B, 2).astype(jnp.int32)
    term_shift = with_ends(jax.random.randint(part_keys[7], (TERMS,), -1, 2), jax.random.fold_in(part_keys[7], 1), -1, 1).astype(jnp.int32)
    return {"wavefunction": wavefunction, "left_blocks": left_blocks, "right_blocks": right_blocks, "site_blocks": site_blocks, "preconditioner": preconditioner, "left_lengths": left_lengths, "right_lengths": right_lengths, "term_shift": term_shift}


def valid_mask(left_lengths, right_lengths):
    offsets = jnp.arange(B, dtype=jnp.int32)
    row_valid = (offsets[None, :] < left_lengths[:, None].astype(jnp.int32)).astype(jnp.float32)
    col_valid = (offsets[None, :] < right_lengths[:, None].astype(jnp.int32)).astype(jnp.float32)
    return row_valid[:, None, :, None] * col_valid[:, None, None, :]

def apply_hamiltonian(vector, left_blocks, right_blocks, site_blocks, term_shift, valid):
    wide_vec = vector.astype(jnp.float32)
    left_groups = left_blocks.reshape(N_OPS, TERM_DEV, NS, B, B)
    right_groups = right_blocks.reshape(N_OPS, TERM_DEV, NS, B, B)
    site_groups = site_blocks.reshape(N_OPS, TERM_DEV, P_SIZE, P_SIZE)
    shift_groups = term_shift.reshape(N_OPS, TERM_DEV)

    def term_step(running, pieces):
        left_piece, right_piece, site_piece, shift_value = pieces
        right_done = jnp.einsum('spac,sdc->spad', wide_vec, right_piece.astype(jnp.float32), precision=lax.Precision.HIGHEST).astype(jnp.bfloat16)
        right_done = lax.optimization_barrier(right_done).astype(jnp.float32)
        applied = jnp.einsum('sab,spbd->spad', left_piece.astype(jnp.float32), right_done, precision=lax.Precision.HIGHEST)
        blended = jnp.einsum('qp,spad->sqad', site_piece, applied, precision=lax.Precision.HIGHEST)
        bucket_slot = (shift_value + 1).astype(jnp.int32)
        current = lax.dynamic_index_in_dim(running, bucket_slot, 0, keepdims=False)
        return (lax.dynamic_update_index_in_dim(running, current + blended, bucket_slot, 0), None)

    def group_step(summed, pieces):
        running, _ = lax.scan(term_step, jnp.zeros((3, NS, P_SIZE, B, B), jnp.float32), pieces)
        rounded = lax.optimization_barrier(running.astype(jnp.bfloat16))
        return (summed + rounded.astype(jnp.float32), None)
    totals, _ = lax.scan(group_step, jnp.zeros((3, NS, P_SIZE, B, B), jnp.float32), (left_groups, right_groups, site_groups, shift_groups))
    falling, staying, rising = (totals[0], totals[1], totals[2])
    blank = jnp.zeros((1, P_SIZE, B, B), jnp.float32)
    moved_rise = jnp.concatenate([blank, rising[:-1]], axis=0)
    moved_fall = jnp.concatenate([falling[1:], blank], axis=0)
    return (staying + moved_rise + moved_fall) * valid

def reference(wavefunction, left_blocks, right_blocks, site_blocks, preconditioner, left_lengths, right_lengths, term_shift):
    valid = valid_mask(left_lengths, right_lengths)
    start = wavefunction * valid.astype(jnp.bfloat16)
    first_sigma = apply_hamiltonian(start, left_blocks, right_blocks, site_blocks, term_shift, valid)
    wide_wave = start.astype(jnp.float32)
    wave_norm = jnp.sum(wide_wave * wide_wave)
    wave_sigma = jnp.sum(wide_wave * first_sigma)
    ritz_value = wave_sigma / wave_norm
    correction = (first_sigma - ritz_value * wide_wave) / preconditioner
    corr_norm = jnp.sum(correction * correction)
    next_vector = (correction * jnp.sqrt(wave_norm / (corr_norm + 1e-06))).astype(jnp.bfloat16)
    second_sigma = apply_hamiltonian(next_vector, left_blocks, right_blocks, site_blocks, term_shift, valid)
    return (first_sigma, second_sigma)
```

```python
import functools

import jax
import jax.numpy as jnp
from jax import lax
from jax.experimental import pallas as pl
from jax.experimental.pallas import tpu as pltpu
from jax.sharding import PartitionSpec as P

F32 = jnp.float32
BF16 = jnp.bfloat16
SUB = 16
CORES = 2
CHUNKS = 4


def kernel(
    n_ops,
    n_bond,
    left_len,
    right_len,
    wave,
    left,
    right,
    site,
    precond,
    out1,
    out2,
    vg,
    lg,
    rg,
    sg,
    mixed,
    xs,
    acc,
    bsend,
    brecv,
    red,
    v_sems,
    vf_sems,
    lr_sib,
    lr_x,
    lr_f,
    site_sems,
    bond_sems,
    red_sems,
):
    terms, sectors, width, _ = left.shape
    mine = wave.shape[1]
    states = vg.shape[1]
    n_x = n_ops // CORES
    per = terms // CHUNKS
    me = lax.axis_index("ops")
    bond = lax.axis_index("bond")
    core = lax.rem(me, CORES)
    chip = me // CORES
    sibling = me + 1 - 2 * core

    def ops_at(offset):
        return lax.rem(me + offset, n_ops)

    def bond_at(offset):
        return lax.rem(bond + offset, n_bond)

    def same_core(offset):
        return lax.rem(chip + offset, n_x) * CORES + core

    def remote(src, dst, sems, target):
        return pltpu.make_async_remote_copy(
            src_ref=src,
            dst_ref=dst,
            send_sem=sems[0],
            recv_sem=sems[1],
            device_id=target,
            device_id_type=pl.DeviceIdType.MESH,
        )

    brecv[...] = jnp.zeros_like(brecv)
    barrier = pltpu.get_barrier_semaphore()
    for j in range(1, n_ops):
        pl.semaphore_signal(barrier, inc=1, device_id={"ops": ops_at(j)}, device_id_type=pl.DeviceIdType.MESH)
    for j in range(1, n_bond):
        pl.semaphore_signal(barrier, inc=1, device_id={"bond": bond_at(j)}, device_id_type=pl.DeviceIdType.MESH)

    rows_at = lax.broadcasted_iota(jnp.int32, (width, width), 0)
    cols_at = lax.broadcasted_iota(jnp.int32, (width, width), 1)

    def valid(s):
        keep = (rows_at < left_len[s]) & (cols_at < right_len[s])
        return jnp.where(keep, 1.0, 0.0).astype(F32)

    own = pl.ds(me * mine, mine)
    norm_part = jnp.zeros((8, width), F32)
    for s in range(sectors):
        keep = valid(s)
        for q in range(mine):
            block = wave[s, q].astype(F32) * keep
            vg[0, me * mine + q, :, s * width : (s + 1) * width] = block.astype(BF16)
            norm_part += jnp.sum((block * block).reshape(width // 8, 8, width), axis=0)
    lg[0] = left[...]
    rg[0] = right[...]
    sg[0] = site[me]

    pl.semaphore_wait(barrier, n_ops - 1 + n_bond - 1)

    def v_copy(turn, offset):
        target = sibling if offset == 0 else same_core(offset)
        where = vg.at[turn, own]
        return remote(
            where, where, (v_sems.at[turn, offset, 0], v_sems.at[turn, offset, 1]), {"ops": target}
        )

    def v_forward(turn, offset):
        owner = same_core(n_x - offset)
        where = vg.at[turn, pl.ds(owner * mine, mine)]
        return remote(
            where, where, (vf_sems.at[turn, offset, 0], vf_sems.at[turn, offset, 1]), {"ops": sibling}
        )

    def start_v(turn):
        for j in range(1, n_x):
            v_copy(turn, j).start()
        v_copy(turn, 0).start()

    def finish_v(turn):
        for j in range(1, n_x):
            v_copy(turn, j).wait_recv()
            v_forward(turn, j).start()
        v_copy(turn, 0).wait_recv()
        for j in range(1, n_x):
            v_forward(turn, j).wait_recv()

    def drain_v(turn):
        for j in range(n_x):
            v_copy(turn, j).wait_send()
        for j in range(1, n_x):
            v_forward(turn, j).wait_send()

    def site_copy(j):
        return remote(
            site.at[ops_at(j)], sg.at[slot_at(j)], (site_sems.at[j, 0], site_sems.at[j, 1]), {"ops": ops_at(j)}
        )

    def slot_at(j):
        there = ops_at(j)
        step = lax.rem(there // CORES - chip + n_x, n_x)
        other = jnp.where(lax.rem(there, CORES) == core, 0, 1)
        return step * CORES + other

    def sib_copy(i):
        src, dst = ((right, rg), (left, lg))[i]
        return remote(src, dst.at[1], (lr_sib.at[i, 0], lr_sib.at[i, 1]), {"ops": sibling})

    def x_copy(offset, chunk, i):
        src, dst = ((right, rg), (left, lg))[i]
        part = pl.ds(chunk * per, per)
        return remote(
            src.at[part],
            dst.at[offset * CORES, part],
            (lr_x.at[offset, chunk, i, 0], lr_x.at[offset, chunk, i, 1]),
            {"ops": same_core(offset)},
        )

    def x_forward(offset, chunk, i):
        dst = (rg, lg)[i]
        part = pl.ds(chunk * per, per)
        return remote(
            dst.at[offset * CORES, part],
            dst.at[offset * CORES + 1, part],
            (lr_f.at[offset, chunk, i, 0], lr_f.at[offset, chunk, i, 1]),
            {"ops": sibling},
        )

    start_v(0)
    for j in range(1, n_ops):
        site_copy(j).start()
    for i in range(2):
        sib_copy(i).start()
    for offset in range(1, n_x):
        for chunk in range(CHUNKS):
            for i in range(2):
                x_copy(offset, chunk, i).start()

    lane = lax.broadcasted_iota(jnp.int32, (SUB, states * SUB), 1)
    sub = lax.broadcasted_iota(jnp.int32, (SUB, states * SUB), 0)
    eye = jnp.where((lane & (SUB - 1)) == sub, 1.0, 0.0).astype(F32)
    count = terms * mine

    def group(turn, slot):
        spread = (sg[slot, :count, :][:, None, :] * eye[None]).astype(BF16)
        spread = spread.reshape(count * SUB, states * SUB)
        for c in range(width // SUB):
            piece = vg[turn, :, c * SUB : (c + 1) * SUB, :].reshape(states * SUB, sectors * width)
            done = jnp.dot(spread, piece, preferred_element_type=F32)
            mixed[:, c * SUB : (c + 1) * SUB, :] = done.astype(BF16).reshape(count, SUB, sectors * width)
        blank = jnp.zeros((width, width), BF16)
        for k in range(terms):
            wide = jnp.concatenate(
                [
                    jnp.concatenate([rg[slot, k, s] if s == u else blank for u in range(sectors)], axis=1)
                    for s in range(sectors)
                ],
                axis=0,
            )
            rows = mixed[k * mine : (k + 1) * mine].reshape(mine * width, sectors * width)
            done = lax.dot_general(
                rows, wide, (((1,), (1,)), ((), ())), preferred_element_type=F32
            ).astype(BF16)
            for q in range(mine):
                for s in range(sectors):
                    xs[s, k * width : (k + 1) * width, q * width : (q + 1) * width] = done[
                        q * width : (q + 1) * width, s * width : (s + 1) * width
                    ]
        for s in range(sectors):
            tall = []
            for d in range(3):
                pieces = []
                for k in range(terms):
                    at = count + d * terms + k
                    flag = sg[slot, at : at + 1, :width].astype(BF16)
                    pieces.append(lg[slot, k, s] * flag)
                tall.append(jnp.concatenate(pieces, axis=1))
            acc[s] += jnp.dot(jnp.concatenate(tall, axis=0), xs[s], preferred_element_type=F32)

    def bond_copy(turn, way):
        target = bond + 1 if way == 0 else bond - 1
        return remote(
            bsend.at[turn, way],
            brecv.at[turn, way],
            (bond_sems.at[turn, way, 0], bond_sems.at[turn, way, 1]),
            {"bond": target},
        )

    last = sectors - 1
    has_next = bond < n_bond - 1
    has_prev = bond > 0

    def exchange(turn):
        bsend[turn, 0] = acc[last, 2 * width :, :].astype(BF16)
        bsend[turn, 1] = acc[0, :width, :].astype(BF16)

        @pl.when(has_next)
        def _():
            bond_copy(turn, 0).start()

        @pl.when(has_prev)
        def _():
            bond_copy(turn, 1).start()

        @pl.when(has_prev)
        def _():
            bond_copy(turn, 0).wait_recv()

        @pl.when(has_next)
        def _():
            bond_copy(turn, 1).wait_recv()

        @pl.when(has_next)
        def _():
            bond_copy(turn, 0).wait_send()

        @pl.when(has_prev)
        def _():
            bond_copy(turn, 1).wait_send()

    def sigma(turn, s, q):
        cols = slice(q * width, (q + 1) * width)
        total = acc[s, width : 2 * width, cols]
        if s > 0:
            total += acc[s - 1, 2 * width :, cols]
        else:
            total += brecv[turn, 0, :, cols].astype(F32)
        if s < last:
            total += acc[s + 1, :width, cols]
        else:
            total += brecv[turn, 1, :, cols].astype(F32)
        return total * valid(s)

    def red_copy(turn, stage, j):
        target = {"ops": ops_at(j)} if stage == 0 else {"bond": bond_at(j)}
        return remote(
            red.at[turn, stage, 0],
            red.at[turn, stage, j],
            (red_sems.at[turn, stage, j, 0], red_sems.at[turn, stage, j, 1]),
            target,
        )

    def red_start(turn, stage, value):
        red[turn, stage, 0] = value
        for j in range(1, (n_ops, n_bond)[stage]):
            red_copy(turn, stage, j).start()

    def red_finish(turn, stage):
        size = (n_ops, n_bond)[stage]
        for j in range(1, size):
            red_copy(turn, stage, j).wait_recv()
        for j in range(1, size):
            red_copy(turn, stage, j).wait_send()
        total = red[turn, stage, 0]
        for j in range(1, size):
            total += red[turn, stage, j]
        return total

    acc[...] = jnp.zeros_like(acc)
    finish_v(0)
    for j in range(1, n_ops):
        site_copy(j).wait_recv()

    def step(slot, carry):
        @pl.when(slot == 1)
        def _():
            for i in range(2):
                sib_copy(i).wait_recv()

        @pl.when((slot >= CORES) & (lax.rem(slot, CORES) == 0))
        def _():
            offset = slot // CORES
            for chunk in range(CHUNKS):
                for i in range(2):
                    x_copy(offset, chunk, i).wait_recv()
                    x_forward(offset, chunk, i).start()

        @pl.when((slot >= CORES) & (lax.rem(slot, CORES) == 1))
        def _():
            offset = slot // CORES
            for chunk in range(CHUNKS):
                for i in range(2):
                    x_forward(offset, chunk, i).wait_recv()

        group(0, slot)
        return carry

    lax.fori_loop(0, n_ops, step, 0)
    exchange(0)
    sig_part = jnp.zeros((8, width), F32)
    for s in range(sectors):
        for q in range(mine):
            block = sigma(0, s, q)
            out1[s, q] = block
            start = vg[0, me * mine + q, :, s * width : (s + 1) * width].astype(F32)
            sig_part += jnp.sum((block * start).reshape(width // 8, 8, width), axis=0)
    red_start(0, 0, jnp.concatenate([norm_part, sig_part], axis=0))
    red_start(0, 1, red_finish(0, 0))
    total = red_finish(0, 1)
    wave_norm = jnp.sum(total[:8])
    ritz = jnp.sum(total[8:]) / wave_norm
    corr_part = jnp.zeros((8, width), F32)
    for s in range(sectors):
        for q in range(mine):
            start = vg[0, me * mine + q, :, s * width : (s + 1) * width].astype(F32)
            corr = (out1[s, q] - ritz * start) / precond[s, q]
            vg[1, me * mine + q, :, s * width : (s + 1) * width] = corr.astype(BF16)
            corr_part += jnp.sum((corr * corr).reshape(width // 8, 8, width), axis=0)
    start_v(1)
    red_start(1, 0, jnp.concatenate([corr_part, corr_part], axis=0))
    acc[...] = jnp.zeros_like(acc)
    finish_v(1)
    red_start(1, 1, red_finish(1, 0))

    def again(slot, carry):
        group(1, slot)
        return carry

    lax.fori_loop(0, n_ops, again, 0)
    corr_norm = jnp.sum(red_finish(1, 1)[:8])
    scale = jnp.sqrt(jnp.full((1, width), wave_norm / (corr_norm + 1e-06), F32))
    exchange(1)
    for s in range(sectors):
        for q in range(mine):
            out2[s, q] = sigma(1, s, q) * scale

    drain_v(0)
    drain_v(1)
    for j in range(1, n_ops):
        site_copy(j).wait_send()
    for i in range(2):
        sib_copy(i).wait_send()
    for offset in range(1, n_x):
        for chunk in range(CHUNKS):
            for i in range(2):
                x_copy(offset, chunk, i).wait_send()
                x_forward(offset, chunk, i).wait_send()


def body(
    n_ops,
    n_bond,
    wavefunction,
    left_blocks,
    right_blocks,
    site_blocks,
    preconditioner,
    left_lengths,
    right_lengths,
    term_shift,
):
    sectors, mine, width, _ = wavefunction.shape
    terms = left_blocks.shape[0]
    states = site_blocks.shape[1]
    lanes = states * SUB
    spread = site_blocks.reshape(terms, n_ops, mine, states).transpose(1, 0, 2, 3)
    spread = jnp.repeat(spread.reshape(n_ops, terms * mine, states), SUB, axis=2)
    flags = (term_shift[None, :] == jnp.arange(-1, 2, dtype=jnp.int32)[:, None]).astype(F32)
    flags = jnp.broadcast_to(flags.reshape(1, 3 * terms, 1), (n_ops, 3 * terms, lanes))
    site = jnp.concatenate([spread, flags], axis=1)
    rows = site.shape[1]
    out = jax.ShapeDtypeStruct((sectors, mine, width, width), F32)
    vmem = pl.BlockSpec(memory_space=pltpu.VMEM)
    smem = pl.BlockSpec(memory_space=pltpu.SMEM)
    n_x = n_ops // CORES
    most = max(n_ops, n_bond)
    dma = pltpu.SemaphoreType.DMA
    first, second = pl.pallas_call(
        functools.partial(kernel, n_ops, n_bond),
        out_shape=(out, out),
        in_specs=[smem, smem] + [vmem] * 5,
        out_specs=(vmem, vmem),
        scratch_shapes=[
            pltpu.VMEM((2, states, width, sectors * width), BF16),
            pltpu.VMEM((n_ops, terms, sectors, width, width), BF16),
            pltpu.VMEM((n_ops, terms, sectors, width, width), BF16),
            pltpu.VMEM((n_ops, rows, lanes), F32),
            pltpu.VMEM((terms * mine, width, sectors * width), BF16),
            pltpu.VMEM((sectors, terms * width, mine * width), BF16),
            pltpu.VMEM((sectors, 3 * width, mine * width), F32),
            pltpu.VMEM((2, 2, width, mine * width), BF16),
            pltpu.VMEM((2, 2, width, mine * width), BF16),
            pltpu.VMEM((2, 2, most, 16, width), F32),
            dma((2, n_x, 2)),
            dma((2, n_x, 2)),
            dma((2, 2)),
            dma((n_x, CHUNKS, 2, 2)),
            dma((n_x, CHUNKS, 2, 2)),
            dma((n_ops, 2)),
            dma((2, 2, 2)),
            dma((2, 2, most, 2)),
        ],
        compiler_params=pltpu.CompilerParams(
            collective_id=0, has_side_effects=True, vmem_limit_bytes=48 * 1024 * 1024
        ),
    )(left_lengths, right_lengths, wavefunction, left_blocks, right_blocks, site, preconditioner)
    return first, second


def solution(mesh):
    in_specs = (
        P(("grp", "bond"), "ops", None, None),
        P(("grp", "ops"), "bond", None, None),
        P(("grp", "ops"), "bond", None, None),
        P(("grp", "ops"), None, None),
        P(("grp", "bond"), "ops", None, None),
        P(("grp", "bond")),
        P(("grp", "bond")),
        P(("grp", "ops")),
    )
    out_specs = (P(("grp", "bond"), "ops", None, None), P(("grp", "bond"), "ops", None, None))
    run = functools.partial(body, mesh.shape["ops"], mesh.shape["bond"])
    return jax.shard_map(run, mesh=mesh, in_specs=in_specs, out_specs=out_specs, check_vma=False)
```

```python
import functools

import jax
import jax.numpy as jnp
from jax import lax
from jax.experimental import pallas as pl
from jax.experimental.pallas import tpu as pltpu
from jax.sharding import PartitionSpec as P

F32 = jnp.float32
BF16 = jnp.bfloat16
SUB = 16
CORES = 2
CHUNKS = 4
FLAT = 0


def kernel(
    n_ops,
    n_bond,
    left_len,
    right_len,
    wave,
    left,
    right,
    site,
    precond,
    out1,
    out2,
    vg,
    lg,
    rg,
    sg,
    mixed,
    xs,
    acc,
    bsend,
    brecv,
    edge,
    pre,
    red,
    v_sems,
    vf_sems,
    lr_sib,
    lr_x,
    lr_f,
    site_sems,
    bond_sems,
    red_sems,
    edge_sems,
    own_sems,
):
    terms, sectors, width, _ = left.shape
    mine = wave.shape[1]
    states = vg.shape[1]
    n_x = n_ops // CORES
    per = terms // CHUNKS
    me = lax.axis_index("ops")
    bond = lax.axis_index("bond")
    core = lax.rem(me, CORES)
    chip = me // CORES
    sibling = me + 1 - 2 * core

    def ops_at(offset):
        return lax.rem(me + offset, n_ops)

    everyone = n_ops * n_bond
    flat = everyone <= FLAT

    def all_at(offset):
        there = lax.rem(bond * n_ops + me + offset, everyone)
        return {"bond": there // n_ops, "ops": lax.rem(there, n_ops)}

    def bond_at(offset):
        return lax.rem(bond + offset, n_bond)

    def same_core(offset):
        return lax.rem(chip + offset, n_x) * CORES + core

    def remote(src, dst, sems, target):
        return pltpu.make_async_remote_copy(
            src_ref=src,
            dst_ref=dst,
            send_sem=sems[0],
            recv_sem=sems[1],
            device_id=target,
            device_id_type=pl.DeviceIdType.MESH,
        )

    brecv[...] = jnp.zeros_like(brecv)
    edge[...] = jnp.zeros_like(edge)
    barrier = pltpu.get_barrier_semaphore()
    if flat:
        for j in range(1, everyone):
            pl.semaphore_signal(barrier, inc=1, device_id=all_at(j), device_id_type=pl.DeviceIdType.MESH)
    else:
        for j in range(1, n_ops):
            pl.semaphore_signal(barrier, inc=1, device_id={"ops": ops_at(j)}, device_id_type=pl.DeviceIdType.MESH)
        for j in range(1, n_bond):
            pl.semaphore_signal(barrier, inc=1, device_id={"bond": bond_at(j)}, device_id_type=pl.DeviceIdType.MESH)
    fetches = [
        pltpu.make_async_copy(src, dst, own_sems.at[i])
        for i, (src, dst) in enumerate(((right, rg.at[0]), (left, lg.at[0]), (precond, pre)))
    ]
    for fetch in fetches:
        fetch.start()

    rows_at = lax.broadcasted_iota(jnp.int32, (width, width), 0)
    cols_at = lax.broadcasted_iota(jnp.int32, (width, width), 1)

    def valid(s):
        keep = (rows_at < left_len[s]) & (cols_at < right_len[s])
        return jnp.where(keep, 1.0, 0.0).astype(F32)

    own = pl.ds(me * mine, mine)
    norm_part = jnp.zeros((8, width), F32)
    for s in range(sectors):
        keep = valid(s)
        for q in range(mine):
            block = wave[s, q].astype(F32) * keep
            vg[0, me * mine + q, :, s * width : (s + 1) * width] = block.astype(BF16)
            norm_part += jnp.sum((block * block).reshape(width // 8, 8, width), axis=0)
    sg[0] = site[me]

    pl.semaphore_wait(barrier, everyone - 1 if flat else n_ops - 1 + n_bond - 1)

    def v_copy(turn, offset):
        target = sibling if offset == 0 else same_core(offset)
        where = vg.at[turn, own]
        return remote(
            where, where, (v_sems.at[turn, offset, 0], v_sems.at[turn, offset, 1]), {"ops": target}
        )

    def v_forward(turn, offset):
        owner = same_core(n_x - offset)
        where = vg.at[turn, pl.ds(owner * mine, mine)]
        return remote(
            where, where, (vf_sems.at[turn, offset, 0], vf_sems.at[turn, offset, 1]), {"ops": sibling}
        )

    def start_v(turn):
        for j in range(1, n_x):
            v_copy(turn, j).start()
        v_copy(turn, 0).start()

    def finish_v(turn):
        for j in range(1, n_x):
            v_copy(turn, j).wait_recv()
            v_forward(turn, j).start()
        v_copy(turn, 0).wait_recv()
        for j in range(1, n_x):
            v_forward(turn, j).wait_recv()

    def drain_v(turn):
        for j in range(n_x):
            v_copy(turn, j).wait_send()
        for j in range(1, n_x):
            v_forward(turn, j).wait_send()

    def site_copy(j):
        return remote(
            site.at[ops_at(j)], sg.at[slot_at(j)], (site_sems.at[j, 0], site_sems.at[j, 1]), {"ops": ops_at(j)}
        )

    def slot_at(j):
        there = ops_at(j)
        step = lax.rem(there // CORES - chip + n_x, n_x)
        other = jnp.where(lax.rem(there, CORES) == core, 0, 1)
        return step * CORES + other

    def sib_copy(i):
        src, dst = ((right, rg), (left, lg))[i]
        return remote(src, dst.at[1], (lr_sib.at[i, 0], lr_sib.at[i, 1]), {"ops": sibling})

    def x_copy(offset, chunk, i):
        src, dst = ((right, rg), (left, lg))[i]
        part = pl.ds(chunk * per, per)
        return remote(
            src.at[part],
            dst.at[offset * CORES, part],
            (lr_x.at[offset, chunk, i, 0], lr_x.at[offset, chunk, i, 1]),
            {"ops": same_core(offset)},
        )

    def x_forward(offset, chunk, i):
        dst = (rg, lg)[i]
        part = pl.ds(chunk * per, per)
        return remote(
            dst.at[offset * CORES, part],
            dst.at[offset * CORES + 1, part],
            (lr_f.at[offset, chunk, i, 0], lr_f.at[offset, chunk, i, 1]),
            {"ops": sibling},
        )

    last = sectors - 1
    has_next = bond < n_bond - 1
    has_prev = bond > 0

    def edge_copy(way):
        at = 0 if way == 0 else last
        return remote(
            vg.at[0, own, :, pl.ds(at * width, width)],
            edge.at[way],
            (edge_sems.at[way, 0], edge_sems.at[way, 1]),
            {"bond": bond - 1 if way == 0 else bond + 1},
        )

    start_v(0)

    @pl.when(has_prev)
    def _():
        edge_copy(0).start()

    @pl.when(has_next)
    def _():
        edge_copy(1).start()

    for j in range(1, n_ops):
        site_copy(j).start()
    for i in range(2):
        sib_copy(i).start()
    for offset in range(1, n_x):
        for chunk in range(CHUNKS):
            for i in range(2):
                x_copy(offset, chunk, i).start()

    lane = lax.broadcasted_iota(jnp.int32, (SUB, states * SUB), 1)
    sub = lax.broadcasted_iota(jnp.int32, (SUB, states * SUB), 0)
    eye = jnp.where((lane & (SUB - 1)) == sub, 1.0, 0.0).astype(F32)
    count = terms * mine

    def group(turn, slot, first, size):
        rows_in = size * mine
        spread = (sg[slot, first * mine : first * mine + rows_in, :][:, None, :] * eye[None]).astype(BF16)
        spread = spread.reshape(rows_in * SUB, states * SUB)
        for c in range(width // SUB):
            piece = vg[turn, :, c * SUB : (c + 1) * SUB, :].reshape(states * SUB, sectors * width)
            done = jnp.dot(spread, piece, preferred_element_type=F32)
            mixed[:rows_in, c * SUB : (c + 1) * SUB, :] = done.astype(BF16).reshape(
                rows_in, SUB, sectors * width
            )
        blank = jnp.zeros((width, width), BF16)
        for k in range(size):
            wide = jnp.concatenate(
                [
                    jnp.concatenate([rg[slot, first + k, s] if s == u else blank for u in range(sectors)], axis=1)
                    for s in range(sectors)
                ],
                axis=0,
            )
            rows = mixed[k * mine : (k + 1) * mine].reshape(mine * width, sectors * width)
            done = lax.dot_general(
                rows, wide, (((1,), (1,)), ((), ())), preferred_element_type=F32
            ).astype(BF16)
            for q in range(mine):
                for s in range(sectors):
                    xs[s, k * width : (k + 1) * width, q * width : (q + 1) * width] = done[
                        q * width : (q + 1) * width, s * width : (s + 1) * width
                    ]
        for s in range(sectors):
            tall = []
            for d in range(3):
                pieces = []
                for k in range(size):
                    at = count + d * terms + first + k
                    flag = sg[slot, at : at + 1, :width].astype(BF16)
                    pieces.append(lg[slot, first + k, s] * flag)
                tall.append(jnp.concatenate(pieces, axis=1))
            acc[s] += jnp.dot(
                jnp.concatenate(tall, axis=0), xs[s, : size * width], preferred_element_type=F32
            )

    def bond_copy(turn, way):
        target = bond + 1 if way == 0 else bond - 1
        return remote(
            bsend.at[turn, way],
            brecv.at[turn, way],
            (bond_sems.at[turn, way, 0], bond_sems.at[turn, way, 1]),
            {"bond": target},
        )

    def exchange_start(turn):
        bsend[turn, 0] = acc[last, 2 * width :, :].astype(BF16)
        bsend[turn, 1] = acc[0, :width, :].astype(BF16)

        @pl.when(has_next)
        def _():
            bond_copy(turn, 0).start()

        @pl.when(has_prev)
        def _():
            bond_copy(turn, 1).start()

    def exchange_finish(turn):
        @pl.when(has_prev)
        def _():
            bond_copy(turn, 0).wait_recv()

        @pl.when(has_next)
        def _():
            bond_copy(turn, 1).wait_recv()

        @pl.when(has_next)
        def _():
            bond_copy(turn, 0).wait_send()

        @pl.when(has_prev)
        def _():
            bond_copy(turn, 1).wait_send()

    def near_sum(s, cols):
        total = acc[s, width : 2 * width, cols]
        if s > 0:
            total += acc[s - 1, 2 * width :, cols]
        if s < last:
            total += acc[s + 1, :width, cols]
        return total

    def sigma(turn, s, q):
        cols = slice(q * width, (q + 1) * width)
        total = near_sum(s, cols)
        if s == 0:
            total += brecv[turn, 0, :, cols].astype(F32)
        if s == last:
            total += brecv[turn, 1, :, cols].astype(F32)
        return total * valid(s)

    def red_copy(turn, stage, j):
        if flat:
            target = all_at(j)
        else:
            target = {"ops": ops_at(j)} if stage == 0 else {"bond": bond_at(j)}
        return remote(
            red.at[turn, stage, 0],
            red.at[turn, stage, j],
            (red_sems.at[turn, stage, j, 0], red_sems.at[turn, stage, j, 1]),
            target,
        )

    def red_start(turn, stage, value):
        red[turn, stage, 0] = value
        for j in range(1, everyone if flat else (n_ops, n_bond)[stage]):
            red_copy(turn, stage, j).start()

    def red_finish(turn, stage):
        size = everyone if flat else (n_ops, n_bond)[stage]
        for j in range(1, size):
            red_copy(turn, stage, j).wait_recv()
        for j in range(1, size):
            red_copy(turn, stage, j).wait_send()
        total = red[turn, stage, 0]
        for j in range(1, size):
            total += red[turn, stage, j]
        return total

    acc[...] = jnp.zeros_like(acc)
    finish_v(0)
    for j in range(1, n_ops):
        site_copy(j).wait_recv()

    fetches[0].wait()
    fetches[1].wait()

    def near(slot, carry):
        @pl.when(slot == 1)
        def _():
            for i in range(2):
                sib_copy(i).wait_recv()

        group(0, slot, 0, terms)
        return carry

    def step(offset, carry):
        for chunk in range(CHUNKS):
            for i in range(2):
                x_copy(offset, chunk, i).wait_recv()
                x_forward(offset, chunk, i).start()
            group(0, offset * CORES, chunk * per, per)
            for i in range(2):
                x_forward(offset, chunk, i).wait_recv()
            group(0, offset * CORES + 1, chunk * per, per)
        return carry

    lax.fori_loop(0, CORES, near, 0)
    lax.fori_loop(1, n_x, step, 0)
    exchange_start(0)
    fetches[2].wait()

    @pl.when(has_next)
    def _():
        edge_copy(0).wait_recv()

    @pl.when(has_prev)
    def _():
        edge_copy(1).wait_recv()

    def fold(block):
        return jnp.sum(block.reshape(width // 8, 8, width), axis=0)

    sig_part = jnp.zeros((8, width), F32)
    for q in range(mine):
        cols = slice(q * width, (q + 1) * width)
        for way in range(2):
            sig_part += fold(bsend[0, way, :, cols].astype(F32) * edge[way, q].astype(F32))
        for s in range(sectors):
            start = vg[0, me * mine + q, :, s * width : (s + 1) * width].astype(F32)
            sig_part += fold(near_sum(s, cols) * start)
    red_start(0, 0, jnp.concatenate([norm_part, sig_part], axis=0))
    if flat:
        total = red_finish(0, 0)
    else:
        red_start(0, 1, red_finish(0, 0))
        total = red_finish(0, 1)
    exchange_finish(0)
    for s in range(sectors):
        for q in range(mine):
            out1[s, q] = sigma(0, s, q)
    wave_norm = jnp.sum(total[:8])
    ritz = jnp.sum(total[8:]) / wave_norm
    corr_part = jnp.zeros((8, width), F32)
    for s in range(sectors):
        for q in range(mine):
            start = vg[0, me * mine + q, :, s * width : (s + 1) * width].astype(F32)
            corr = (out1[s, q] - ritz * start) / pre[s, q]
            vg[1, me * mine + q, :, s * width : (s + 1) * width] = corr.astype(BF16)
            corr_part += jnp.sum((corr * corr).reshape(width // 8, 8, width), axis=0)
    red_start(1, 0, jnp.concatenate([corr_part, corr_part], axis=0))
    start_v(1)
    acc[...] = jnp.zeros_like(acc)
    finish_v(1)
    if not flat:
        red_start(1, 1, red_finish(1, 0))

    def again(slot, carry):
        group(1, slot, 0, terms)
        return carry

    lax.fori_loop(0, n_ops, again, 0)
    exchange_start(1)
    corr_norm = jnp.sum(red_finish(1, 0 if flat else 1)[:8])
    scale = jnp.sqrt(jnp.full((1, width), wave_norm / (corr_norm + 1e-06), F32))
    exchange_finish(1)
    for s in range(sectors):
        for q in range(mine):
            out2[s, q] = sigma(1, s, q) * scale


    @pl.when(has_prev)
    def _():
        edge_copy(0).wait_send()

    @pl.when(has_next)
    def _():
        edge_copy(1).wait_send()

    drain_v(0)
    drain_v(1)
    for j in range(1, n_ops):
        site_copy(j).wait_send()
    for i in range(2):
        sib_copy(i).wait_send()
    for offset in range(1, n_x):
        for chunk in range(CHUNKS):
            for i in range(2):
                x_copy(offset, chunk, i).wait_send()
                x_forward(offset, chunk, i).wait_send()


def body(
    n_ops,
    n_bond,
    wavefunction,
    left_blocks,
    right_blocks,
    site_blocks,
    preconditioner,
    left_lengths,
    right_lengths,
    term_shift,
):
    sectors, mine, width, _ = wavefunction.shape
    terms = left_blocks.shape[0]
    states = site_blocks.shape[1]
    lanes = states * SUB
    spread = site_blocks.reshape(terms, n_ops, mine, states).transpose(1, 0, 2, 3)
    spread = jnp.repeat(spread.reshape(n_ops, terms * mine, states), SUB, axis=2)
    flags = (term_shift[None, :] == jnp.arange(-1, 2, dtype=jnp.int32)[:, None]).astype(F32)
    flags = jnp.broadcast_to(flags.reshape(1, 3 * terms, 1), (n_ops, 3 * terms, lanes))
    site = jnp.concatenate([spread, flags], axis=1)
    rows = site.shape[1]
    out = jax.ShapeDtypeStruct((sectors, mine, width, width), F32)
    vmem = pl.BlockSpec(memory_space=pltpu.VMEM)
    far = pl.BlockSpec(memory_space=pl.ANY)
    smem = pl.BlockSpec(memory_space=pltpu.SMEM)
    n_x = n_ops // CORES
    most = n_ops * n_bond if n_ops * n_bond <= FLAT else max(n_ops, n_bond)
    dma = pltpu.SemaphoreType.DMA
    first, second = pl.pallas_call(
        functools.partial(kernel, n_ops, n_bond),
        out_shape=(out, out),
        in_specs=[smem, smem, vmem, far, far, vmem, far],
        out_specs=(vmem, vmem),
        scratch_shapes=[
            pltpu.VMEM((2, states, width, sectors * width), BF16),
            pltpu.VMEM((n_ops, terms, sectors, width, width), BF16),
            pltpu.VMEM((n_ops, terms, sectors, width, width), BF16),
            pltpu.VMEM((n_ops, rows, lanes), F32),
            pltpu.VMEM((terms * mine, width, sectors * width), BF16),
            pltpu.VMEM((sectors, terms * width, mine * width), BF16),
            pltpu.VMEM((sectors, 3 * width, mine * width), F32),
            pltpu.VMEM((2, 2, width, mine * width), BF16),
            pltpu.VMEM((2, 2, width, mine * width), BF16),
            pltpu.VMEM((2, mine, width, width), BF16),
            pltpu.VMEM((sectors, mine, width, width), F32),
            pltpu.VMEM((2, 2, most, 16, width), F32),
            dma((2, n_x, 2)),
            dma((2, n_x, 2)),
            dma((2, 2)),
            dma((n_x, CHUNKS, 2, 2)),
            dma((n_x, CHUNKS, 2, 2)),
            dma((n_ops, 2)),
            dma((2, 2, 2)),
            dma((2, 2, most, 2)),
            dma((2, 2)),
            dma((3,)),
        ],
        compiler_params=pltpu.CompilerParams(
            collective_id=0, has_side_effects=True, vmem_limit_bytes=48 * 1024 * 1024
        ),
    )(left_lengths, right_lengths, wavefunction, left_blocks, right_blocks, site, preconditioner)
    return first, second


def solution(mesh):
    in_specs = (
        P(("grp", "bond"), "ops", None, None),
        P(("grp", "ops"), "bond", None, None),
        P(("grp", "ops"), "bond", None, None),
        P(("grp", "ops"), None, None),
        P(("grp", "bond"), "ops", None, None),
        P(("grp", "bond")),
        P(("grp", "bond")),
        P(("grp", "ops")),
    )
    out_specs = (P(("grp", "bond"), "ops", None, None), P(("grp", "bond"), "ops", None, None))
    run = functools.partial(body, mesh.shape["ops"], mesh.shape["bond"])
    return jax.shard_map(run, mesh=mesh, in_specs=in_specs, out_specs=out_specs, check_vma=False)
```
